32 devices in a mesh: seq: 8 (over y, x, core), head: 4 (over z).
Axes of the slice: x: 2, y: 2, z: 4, core: 2. Of those that a mesh axis runs over, the one named last changes fastest.
Arguments:
- d_bytes: bfloat16 [2048, 8192], P('seq', 'head'), may hold values from -6 to 6
- owner_groups: int32 [8, 8], replicated, may hold values from 0 to 63, as said below
- block_order: int32 [8], replicated, may hold values from 0 to 7, each once
- y_in: bfloat16 [2048, 4096], P('seq'), may hold values from -0.29882812 to 0.29882812
- w_proj: bfloat16 [4096, 8192], P('seq', 'head'), may hold values from -0.0625 to 0.0625
- w_out: bfloat16 [2048, 4096], P('head', 'seq'), may hold values from -0.125 to 0.125
- queries: bfloat16 [2048, 2048], P('seq', 'head'), may hold values from -24 to 24
- keys: bfloat16 [2048, 2048], P('seq', 'head'), may hold values from -24 to 24
- values: bfloat16 [2048, 2048], P('seq', 'head'), may hold values from -6 to 6
- attn_out: bfloat16 [2048, 2048], P('seq', 'head'), may hold values from -0.59765625 to 0.59765625
Outputs:
- layer_grad: bfloat16 [2048, 4096], P('seq', 'head')
- grad_proj: bfloat16 [4096, 8192], P('seq', 'head')
- grad_out: bfloat16 [2048, 4096], P('head', 'seq')
- grad_queries: bfloat16 [2048, 2048], P('seq', 'head')
- grad_keys: bfloat16 [2048, 2048], P('seq', 'head')
- grad_values: bfloat16 [2048, 2048], P('seq', 'head')
The draws below stay inside these ranges and needn't reach their ends.
Inputs may be any that keep to these rules, and one draw needn't show every extreme that they name: `owner_groups`: row o lists the patch groups held by owner o; it holds exactly one group of every seq shard (group g covers patches g * 32 to g * 32 + 31, shard g // 8), and every group appears once. `block_order`: A permutation.
All inputs are finite; a program needn't handle non-finite values.
Results may differ from the reference program's by a relative error of at most 0.03.
Values may be sent and summed in bfloat16 or wider, within the bound.
A program may use at most 128 MiB of HBM per device.

```python
import math
import jax
import jax.numpy as jnp
from jax import lax

D = 4096
HEADS = 16
HEAD_DIM = 128
PATCH_DEV = 256
BYTE_W = 8192
HW = 2048
PATCHES = 2048
OWNERS = 8
SPLITS = 4
GROUP = 32


def draw_pair(key):
    key_query = jax.random.fold_in(key, 11)
    key_key = jax.random.fold_in(key, 12)
    query_all = jax.random.normal(key_query, (PATCHES, HW), jnp.float32)
    key_all = jax.random.normal(key_key, (PATCHES, HW), jnp.float32)
    query_all = jnp.clip(query_all, -6.0, 6.0)
    key_all = jnp.clip(key_all, -6.0, 6.0)
    return (query_all, key_all)


def draw_queries(key, part):
    return draw_pair(key)[0].astype(jnp.bfloat16)


def draw_keys(key, part):
    return draw_pair(key)[1].astype(jnp.bfloat16)


def draw_owner_groups(key, part):
    shard_keys = jax.random.split(jax.random.fold_in(key, 21), OWNERS)
    placed = jax.vmap(lambda single: jax.random.permutation(single, OWNERS))(shard_keys)
    inverse = jnp.argsort(placed, axis=1).astype(jnp.int32)
    identity = jnp.arange(OWNERS, dtype=jnp.int32)[:, None] * OWNERS + inverse
    table = identity.T
    owner_keys = jax.random.split(jax.random.fold_in(key, 22), OWNERS)
    shuffle = jax.vmap(lambda single: jax.random.permutation(single, OWNERS))(owner_keys).astype(jnp.int32)
    return jnp.take_along_axis(table, shuffle, axis=1).astype(jnp.int32)


def block_scale(own_key, shape, cuts, least, high):
    factor_of = 1.0
    for dim, shards_of in cuts:
        heights = jax.random.uniform(jax.random.fold_in(jax.random.fold_in(own_key, 6), dim), (shards_of,), jnp.float32, least / len(cuts), high / len(cuts))
        factor_of = factor_of * jnp.repeat(jnp.exp(heights), shape[dim] // shards_of).reshape((-1,) + (1,) * (len(shape) - 1 - dim))
    return factor_of


def bell_draw(rng, extent, deviation, limit, shards=(), held_as=jnp.bfloat16):
    result = jax.random.normal(rng, extent, jnp.float32) * deviation
    if len(shards) > 0:
        result = block_scale(rng, extent, shards, -0.22, 0.18) * result
    return jnp.clip(result, min=-limit, max=limit).astype(held_as)


def setup_inputs(seed: int = 0) -> dict:
    arg_keys = jax.random.split(jax.random.key(seed), 11)
    return {
        "d_bytes": bell_draw(arg_keys[0], (PATCHES, BYTE_W), 1.0, 6.0, ((0, 8), (1, 4))),
        "owner_groups": draw_owner_groups(jax.random.fold_in(arg_keys[10], 71), 0),
        "block_order": jax.random.permutation(arg_keys[2], OWNERS).astype(jnp.int32),
        "y_in": bell_draw(arg_keys[3], (PATCHES, D), 0.05, 0.29882812, ((0, 8),)),
        "w_proj": bell_draw(arg_keys[4], (D, BYTE_W), BYTE_W ** -0.5, 0.0625, ((0, 8), (1, 4))),
        "w_out": bell_draw(arg_keys[5], (HW, D), HW ** -0.5, 0.125, ((0, 4), (1, 8))),
        "queries": draw_queries(jax.random.fold_in(arg_keys[10], 71), 0),
        "keys": draw_keys(jax.random.fold_in(arg_keys[10], 71), 0),
        "values": bell_draw(arg_keys[8], (PATCHES, HW), 1.0, 6.0, ((0, 8), (1, 4))),
        "attn_out": bell_draw(arg_keys[9], (PATCHES, HW), 0.1, 0.59765625, ((0, 8), (1, 4))),
    }


def reference(d_bytes, owner_groups, block_order, y_in, w_proj, w_out, queries, keys, values, attn_out):
    flt = jnp.float32
    half = jnp.bfloat16
    flat_ids = owner_groups.reshape(-1)
    inverse = jnp.argsort(flat_ids).astype(jnp.int32)
    owned = d_bytes.reshape(OWNERS * OWNERS, GROUP, BYTE_W)
    natural = jnp.take(owned, inverse, axis=0).reshape(PATCHES, BYTE_W)
    grad_proj = lax.dot_general(y_in, natural, (((0,), (0,)), ((), ())), preferred_element_type=flt).astype(half)
    width = BYTE_W // SPLITS
    summed = jnp.zeros((PATCHES, D), flt)
    for column_group in range(SPLITS):
        lower = column_group * width
        portion = lax.dot_general(natural[:, lower:lower + width], w_proj[:, lower:lower + width], (((1,), (1,)), ((), ())), preferred_element_type=flt)
        summed = summed + lax.optimization_barrier(portion.astype(half)).astype(flt)
    layer_grad = summed.astype(half)
    attn_grad = lax.dot_general(layer_grad, w_out, (((1,), (1,)), ((), ())), preferred_element_type=flt).astype(half)
    out_sum = jnp.zeros((HW, D), flt)
    for shard_index in range(OWNERS):
        lower = shard_index * PATCH_DEV
        portion = lax.dot_general(attn_out[lower:lower + PATCH_DEV], layer_grad[lower:lower + PATCH_DEV], (((0,), (0,)), ((), ())), preferred_element_type=flt)
        out_sum = out_sum + lax.optimization_barrier(portion.astype(half)).astype(flt)
    grad_out = out_sum.astype(half)
    rows = jnp.arange(PATCHES, dtype=jnp.int32)
    position = block_order[rows // PATCH_DEV] * PATCH_DEV + rows % PATCH_DEV
    scale = 1.0 / math.sqrt(HEAD_DIM)
    key_heads = keys.astype(flt).reshape(PATCHES, HEADS, HEAD_DIM)
    value_heads = values.astype(flt).reshape(PATCHES, HEADS, HEAD_DIM)

    def shard(running, shard_index):
        key_sum, value_sum = running
        lower = shard_index * PATCH_DEV
        query_now = lax.dynamic_slice_in_dim(queries, lower, PATCH_DEV, 0).astype(flt).reshape(PATCH_DEV, HEADS, HEAD_DIM)
        grad_now = lax.dynamic_slice_in_dim(attn_grad, lower, PATCH_DEV, 0).astype(flt).reshape(PATCH_DEV, HEADS, HEAD_DIM)
        output_now = lax.dynamic_slice_in_dim(attn_out, lower, PATCH_DEV, 0).astype(flt).reshape(PATCH_DEV, HEADS, HEAD_DIM)
        query_pos = lax.dynamic_slice_in_dim(position, lower, PATCH_DEV, 0)
        allowed = position[None, :] <= query_pos[:, None]
        scores = jnp.einsum('qhd,khd->hqk', query_now, key_heads) * scale
        scores = jnp.where(allowed[None], scores, -jnp.inf)
        highest = lax.optimization_barrier(jnp.max(scores, axis=2, keepdims=True))
        log_total = highest + jnp.log(lax.optimization_barrier(jnp.sum(jnp.exp(scores - highest), axis=2, keepdims=True)))
        weights = jnp.exp(scores - log_total)
        delta = lax.optimization_barrier(jnp.sum(grad_now * output_now, axis=2)).T[:, :, None]
        grad_weights = jnp.einsum('qhd,khd->hqk', grad_now, value_heads)
        grad_scores = lax.optimization_barrier((weights * (grad_weights - delta) * scale).astype(half)).astype(flt)
        weights_low = lax.optimization_barrier(weights.astype(half)).astype(flt)
        grad_query = jnp.einsum('hqk,khd->qhd', grad_scores, key_heads).reshape(PATCH_DEV, HW).astype(half)
        key_term = jnp.einsum('hqk,qhd->khd', grad_scores, query_now).reshape(PATCHES, HW)
        value_term = jnp.einsum('hqk,qhd->khd', weights_low, grad_now).reshape(PATCHES, HW)
        key_sum = key_sum + lax.optimization_barrier(key_term.astype(half)).astype(flt)
        value_sum = value_sum + lax.optimization_barrier(value_term.astype(half)).astype(flt)
        return ((key_sum, value_sum), grad_query)
    start_state = (jnp.zeros((PATCHES, HW), flt), jnp.zeros((PATCHES, HW), flt))
    (key_sum, value_sum), query_grads = lax.scan(shard, start_state, jnp.arange(OWNERS, dtype=jnp.int32))
    grad_queries = query_grads.reshape(PATCHES, HW)
    return (layer_grad, grad_proj, grad_out, grad_queries, key_sum.astype(half), value_sum.astype(half))
```

```python
import functools
import math

import jax
import jax.numpy as jnp
from jax import lax
from jax.experimental import pallas as pl
from jax.experimental.pallas import tpu as pltpu
from jax.sharding import PartitionSpec as P

HEAD_DIM = 128
MESH = pl.DeviceIdType.MESH
FLT = jnp.float32
HALF = jnp.bfloat16
ANY = pl.BlockSpec(memory_space=pl.ANY)
VMEM = pl.BlockSpec(memory_space=pltpu.VMEM)
SMEM = pl.BlockSpec(memory_space=pltpu.SMEM)
VMEM_LIMIT = 56 * 1024 * 1024


def greet(axes):
    barrier = pltpu.get_barrier_semaphore()
    count = 0
    for axis, size in axes:
        me = lax.axis_index(axis)
        for k in range(1, size):
            pl.semaphore_signal(
                barrier, inc=1, device_id={axis: lax.rem(me + k, size)}, device_id_type=MESH
            )
        count += size - 1
    pl.semaphore_wait(barrier, count)


def spread(stride, n, source, target, send, recv):
    me = lax.axis_index("seq")
    size = n // stride
    copies = []
    for k in range(1, size):
        dst = lax.rem(me // stride + k, size) * stride + lax.rem(me, stride)
        copy = pltpu.make_async_remote_copy(
            src_ref=source(dst),
            dst_ref=target,
            send_sem=send.at[k],
            recv_sem=recv.at[k],
            device_id={"seq": dst},
            device_id_type=MESH,
        )
        copy.start()
        copies.append(copy)
    own = pltpu.make_async_copy(source(me), target, recv.at[0])
    own.start()
    return copies + [own]


def gather_kernel(n, d_ref, out_ref, send, recv, pair_send, pair_recv):
    me = lax.axis_index("seq")
    chips = n // 2
    chip, core = me // 2, lax.rem(me, 2)
    other = chip * 2 + (1 - core)
    greet((("seq", n),))
    copies = spread(2, n, lambda dst: d_ref, out_ref.at[me], send, recv)

    def pass_on(k, source, slot):
        copy = pltpu.make_async_remote_copy(
            src_ref=source,
            dst_ref=out_ref.at[slot],
            send_sem=pair_send.at[k],
            recv_sem=pair_recv.at[k],
            device_id={"seq": other},
            device_id_type=MESH,
        )
        copy.start()
        return copy

    passed = [pass_on(0, d_ref, me)]
    for k in range(1, chips):
        copies[k - 1].wait_recv()
        slot = lax.rem(chip + chips - k, chips) * 2 + core
        passed.append(pass_on(k, out_ref.at[slot], slot))
    for copy in passed:
        copy.wait()
    for copy in copies[:-1]:
        copy.wait_send()
    copies[-1].wait()


def gather(d_bytes, n):
    chips = n // 2
    return pl.pallas_call(
        functools.partial(gather_kernel, n),
        out_shape=jax.ShapeDtypeStruct((n,) + d_bytes.shape, d_bytes.dtype),
        in_specs=[ANY],
        out_specs=ANY,
        scratch_shapes=[pltpu.SemaphoreType.DMA((chips,))] * 4,
        compiler_params=pltpu.CompilerParams(collective_id=1, has_side_effects=True),
    )(d_bytes)


def middle_kernel(
    n, splits, heads, chunks,
    part, y, q, k, v, o,
    grad, y_all, q_all, k_all, v_all, o_all, oq_all,
    outer_buf, pair_buf, middle_buf, total,
    y_s, y_r, q_s, q_r, k_s, k_r, v_s, v_r, o_s, o_r, p_s, p_r, a_s, a_r, b_s, b_r, c_s, c_r,
):
    me = lax.axis_index("seq")
    z = lax.axis_index("head")
    share = n // heads
    greet((("seq", n), ("head", splits)) if splits == 4 else (("seq", n),))
    rows = part.shape[0] // chunks
    inner = jnp.logical_and(z >= 1, z <= 2)
    outer = jnp.logical_not(inner)
    beside = (z // 2) * 2 + (1 - lax.rem(z, 2))
    across = 3 - z

    def send(source, target, s, r, c, to):
        here = pl.ds(c * rows, rows)
        return pltpu.make_async_remote_copy(
            src_ref=source.at[here],
            dst_ref=target.at[here],
            send_sem=s.at[c],
            recv_sem=r.at[c],
            device_id={"head": to},
            device_id_type=MESH,
        )

    line = splits == 4
    first = [send(part, outer_buf, a_s, a_r, c, beside) for c in range(chunks)]
    second = [send(pair_buf, middle_buf, b_s, b_r, c, across) for c in range(chunks)]
    third = [send(total, total, c_s, c_r, c, beside) for c in range(chunks)]

    if line:

        @pl.when(outer)
        def _():
            for copy in first:
                copy.start()

    width = y.shape[1] // n

    def columns(ref, size, index):
        return ref.at[:, pl.ds(pl.multiple_of(index * size, size), size)]

    copies = spread(share, n, lambda d: columns(q, HEAD_DIM, d // share), q_all.at[me // share], q_s, q_r)
    copies += spread(share, n, lambda d: columns(o, HEAD_DIM, d // share), oq_all.at[me // share], p_s, p_r)
    copies += spread(1, n, lambda d: o, o_all.at[me], o_s, o_r)
    copies += spread(1, n, lambda d: columns(k, HEAD_DIM, d // share), k_all.at[me], k_s, k_r)
    copies += spread(1, n, lambda d: columns(v, HEAD_DIM, d // share), v_all.at[me], v_s, v_r)
    copies += spread(1, n, lambda d: columns(y, width, d), y_all.at[me], y_s, y_r)

    if line:

        @pl.when(inner)
        def _():
            lag = 2
            for step in range(chunks + lag):
                if step < chunks:
                    here = pl.ds(step * rows, rows)
                    first[step].wait_recv()
                    pair_buf[here] = (part[here].astype(FLT) + outer_buf[here].astype(FLT)).astype(HALF)
                    second[step].start()
                if step >= lag:
                    c = step - lag
                    here = pl.ds(c * rows, rows)
                    second[c].wait_recv()
                    total[here] = (pair_buf[here].astype(FLT) + middle_buf[here].astype(FLT)).astype(HALF)
                    third[c].start()
            for c in range(chunks):
                second[c].wait_send()
                third[c].wait_send()

        @pl.when(outer)
        def _():
            for c in range(chunks):
                third[c].wait_recv()
            for c in range(chunks):
                first[c].wait_send()

        grad[...] = total[...]
    else:
        grad[...] = part[...]
    for copy in copies:
        copy.wait()


def middle(part, y, q, k, v, o, n, splits):
    heads = q.shape[1] // HEAD_DIM
    rows = y.shape[0]
    chunks = 8
    block = lambda m, w: jax.ShapeDtypeStruct((m, rows, w), HALF)
    dma = pltpu.SemaphoreType.DMA
    return pl.pallas_call(
        functools.partial(middle_kernel, n, splits, heads, chunks),
        out_shape=(
            jax.ShapeDtypeStruct(part.shape, HALF),
            block(n, y.shape[1] // n),
            block(heads, HEAD_DIM),
            block(n, HEAD_DIM),
            block(n, HEAD_DIM),
            block(n, o.shape[1]),
            block(heads, HEAD_DIM),
        ),
        in_specs=[VMEM] + [ANY] * 5,
        out_specs=[VMEM] + [ANY] * 6,
        scratch_shapes=[pltpu.VMEM(part.shape, HALF)] * 4
        + [dma((n,))] * 12
        + [dma((chunks,))] * 6,
        compiler_params=pltpu.CompilerParams(
            collective_id=2, has_side_effects=True, vmem_limit_bytes=VMEM_LIMIT
        ),
    )(part, y, q, k, v, o)


def scatter_kernel(n, share, a_ref, out_ref, send, recv):
    me = lax.axis_index("seq")
    greet((("seq", n),))

    def source(d):
        column = pl.ds(pl.multiple_of(d // share * HEAD_DIM, HEAD_DIM), HEAD_DIM)
        return a_ref.at[:, lax.rem(d, share), :, column]

    for copy in spread(1, n, source, out_ref.at[me], send, recv):
        copy.wait()


def scatter(partial, n, share):
    slots, rows = partial.shape[0], partial.shape[2]
    return pl.pallas_call(
        functools.partial(scatter_kernel, n, share),
        out_shape=jax.ShapeDtypeStruct((n, slots, rows, HEAD_DIM), HALF),
        in_specs=[ANY],
        out_specs=ANY,
        scratch_shapes=[pltpu.SemaphoreType.DMA((n,))] * 2,
        compiler_params=pltpu.CompilerParams(collective_id=3, has_side_effects=True),
    )(partial)


def return_kernel(
    n, share, per, dq, dk, dv, grad, dq_out, dk_out, dv_out, grad_out, q_s, q_r, k_s, k_r, v_s, v_r, g_s, g_r
):
    me = lax.axis_index("seq")
    c = lax.axis_index("head")
    greet((("seq", n),))
    slot = lax.rem(me, per)
    sends = me // per == c
    shares = []
    for k in range(1, n):
        dst = lax.rem(me + k, n)
        shares.append(
            pltpu.make_async_remote_copy(
                src_ref=grad.at[dst],
                dst_ref=grad_out.at[slot],
                send_sem=g_s.at[k],
                recv_sem=g_r.at[slot],
                device_id={"seq": dst},
                device_id_type=MESH,
            )
        )
    own = pltpu.make_async_copy(grad.at[me], grad_out.at[slot], g_s.at[0])

    @pl.when(sends)
    def _():
        own.start()
        for copy in shares:
            copy.start()

    copies = spread(share, n, lambda d: dq.at[d // share], dq_out.at[me // share], q_s, q_r)
    copies += spread(1, n, lambda d: dk.at[d], dk_out.at[me], k_s, k_r)
    copies += spread(1, n, lambda d: dv.at[d], dv_out.at[me], v_s, v_r)
    for copy in copies:
        copy.wait()

    @pl.when(sends)
    def _():
        own.wait()
        for copy in shares:
            copy.wait_send()

    for i in range(per):

        @pl.when(c * per + i != me)
        def _():
            pltpu.make_async_copy(grad.at[0], grad_out.at[i], g_r.at[i]).wait()


def send_back(dq, dk, dv, grad, n, share, splits):
    per = n // splits
    dma = pltpu.SemaphoreType.DMA
    return pl.pallas_call(
        functools.partial(return_kernel, n, share, per),
        out_shape=(
            jax.ShapeDtypeStruct(dq.shape, HALF),
            jax.ShapeDtypeStruct(dk.shape, HALF),
            jax.ShapeDtypeStruct(dv.shape, HALF),
            jax.ShapeDtypeStruct((per,) + grad.shape[1:], HALF),
        ),
        in_specs=[ANY] * 4,
        out_specs=[ANY] * 4,
        scratch_shapes=[dma((n,))] * 7 + [dma((per,))],
        compiler_params=pltpu.CompilerParams(collective_id=4, has_side_effects=True),
    )(dq, dk, dv, grad)


def fetch_natural(groups, d_ref, nat, sem):
    owners, slots = groups.shape
    size = nat.shape[0] // (owners * slots)

    @pl.loop(0, owners)
    def _(o):
        for j in range(slots):
            g = groups[o, j]
            pltpu.make_async_copy(
                d_ref.at[o, pl.ds(j * size, size)],
                nat.at[pl.ds(pl.multiple_of(g * size, size), size)],
                sem,
            ).start()


def natural_done(nat, sem):
    pltpu.make_async_copy(nat, nat, sem).wait()


def part_kernel(groups, d_ref, w, out, nat, sem):
    fetch_natural(groups, d_ref, nat, sem)
    natural_done(nat, sem)
    tile = 256

    @pl.loop(0, nat.shape[0] // tile)
    def _(i):
        here = pl.ds(pl.multiple_of(i * tile, tile), tile)
        out[here] = lax.dot_general(
            nat[here], w[...], (((1,), (1,)), ((), ())), preferred_element_type=FLT
        ).astype(HALF)


def proj_kernel(groups, d_ref, y, out, nat, sem):
    fetch_natural(groups, d_ref, nat, sem)
    natural_done(nat, sem)
    tile = 512

    @pl.loop(0, nat.shape[1] // tile)
    def _(i):
        here = pl.ds(pl.multiple_of(i * tile, tile), tile)
        out[:, here] = lax.dot_general(
            y[...], nat[:, here], (((0,), (0,)), ((), ())), preferred_element_type=FLT
        ).astype(HALF)


def with_natural(kernel, groups, d_all, other, out_shape):
    nat = (d_all.shape[0] * d_all.shape[1], d_all.shape[2])
    return pl.pallas_call(
        kernel,
        out_shape=jax.ShapeDtypeStruct(out_shape, HALF),
        in_specs=[SMEM, ANY, VMEM],
        out_specs=VMEM,
        scratch_shapes=[pltpu.VMEM(nat, HALF), pltpu.SemaphoreType.DMA],
        compiler_params=pltpu.CompilerParams(vmem_limit_bytes=VMEM_LIMIT),
    )(groups, d_all, other)


def attention_kernel(qpos, kpos, q, k, v, o, go, dq, dk, dv, dk_sum, dv_sum):
    j = pl.program_id(0)
    scale = 1.0 / math.sqrt(HEAD_DIM)

    @pl.when(j == 0)
    def _():
        dk_sum[...] = jnp.zeros_like(dk_sum)
        dv_sum[...] = jnp.zeros_like(dv_sum)

    g = jnp.sum(go[:, 0].astype(FLT), axis=0).astype(HALF)
    delta = jnp.sum(g.astype(FLT) * o[0].astype(FLT), axis=1, keepdims=True)
    rowwise = (((1,), (1,)), ((), ()))
    columnwise = (((0,), (0,)), ((), ()))
    s = lax.dot_general(q[0], k[...], rowwise, preferred_element_type=FLT) * scale
    s = jnp.where(kpos[...] <= qpos[0], s, -1e30)
    high = jnp.max(s, axis=1, keepdims=True)
    e = jnp.exp(s - high)
    p = e * (1.0 / jnp.sum(e, axis=1, keepdims=True))
    dp = lax.dot_general(g, v[...], rowwise, preferred_element_type=FLT)
    ds = (p * (dp - delta) * scale).astype(HALF)
    low = p.astype(HALF)
    dq[0] = jnp.dot(ds, k[...], preferred_element_type=FLT).astype(HALF)
    dk_sum[...] += lax.dot_general(ds, q[0], columnwise, preferred_element_type=FLT)
    dv_sum[...] += lax.dot_general(low, g, columnwise, preferred_element_type=FLT)

    @pl.when(j == pl.num_programs(0) - 1)
    def _():
        dk[...] = dk_sum[...].astype(HALF)
        dv[...] = dv_sum[...].astype(HALF)


def attention(qpos, kpos, q, k, v, o, go):
    slots, rows, _ = q.shape
    n = go.shape[0]
    every = k.shape
    block = pl.BlockSpec((1, rows, HEAD_DIM), lambda j: (j, 0, 0))
    whole = pl.BlockSpec(every, lambda j: (0, 0))
    return pl.pallas_call(
        attention_kernel,
        grid=(slots,),
        out_shape=(
            jax.ShapeDtypeStruct(q.shape, HALF),
            jax.ShapeDtypeStruct(every, HALF),
            jax.ShapeDtypeStruct(every, HALF),
        ),
        in_specs=[
            pl.BlockSpec((1, rows, 1), lambda j: (j, 0, 0)),
            pl.BlockSpec(kpos.shape, lambda j: (0, 0)),
            block,
            whole,
            whole,
            block,
            pl.BlockSpec((n, 1, rows, HEAD_DIM), lambda j: (0, j, 0, 0)),
        ],
        out_specs=[block, whole, whole],
        scratch_shapes=[pltpu.VMEM(every, FLT)] * 2,
        compiler_params=pltpu.CompilerParams(vmem_limit_bytes=VMEM_LIMIT),
    )(qpos, kpos, q, k, v, o, go)


def body(d_bytes, owner_groups, block_order, y_in, w_proj, w_out, queries, keys, values, attn_out):
    n = lax.axis_size("seq")
    splits = lax.axis_size("head")
    me = lax.axis_index("seq")
    rows, width = queries.shape
    heads = width // HEAD_DIM
    share = n // heads
    patches = n * rows
    features = w_proj.shape[0]

    d_all = gather(d_bytes, n)
    part = with_natural(part_kernel, owner_groups, d_all, w_proj, (patches, features))
    if splits != 4:
        part = lax.psum(part, "head")
    grad, y_all, q_all, k_all, v_all, o_all, oq_all = middle(
        part, y_in, queries, keys, values, attn_out, n, splits
    )
    partial = lax.dot_general(
        grad, w_out, (((1,), (1,)), ((), ())), preferred_element_type=FLT
    ).astype(HALF)
    go = scatter(partial.reshape(heads, share, rows, width), n, share)
    grad_out = lax.dot_general(
        o_all.reshape(patches, width), grad, (((0,), (0,)), ((), ())), preferred_element_type=FLT
    ).astype(HALF)
    grad_proj = with_natural(
        proj_kernel, owner_groups, d_all, y_all.reshape(patches, features), (features, d_bytes.shape[1])
    )
    pos = block_order[:, None] * rows + jnp.arange(rows, dtype=jnp.int32)[None, :]
    mine = lax.dynamic_index_in_dim(pos.reshape(heads, share, rows), lax.rem(me, share), 1, False)
    dq, dk, dv = attention(
        mine[:, :, None],
        pos.reshape(1, patches),
        q_all,
        k_all.reshape(patches, HEAD_DIM),
        v_all.reshape(patches, HEAD_DIM),
        oq_all,
        go,
    )
    dq, dk, dv, grad = send_back(
        dq,
        dk.reshape(n, rows, HEAD_DIM),
        dv.reshape(n, rows, HEAD_DIM),
        grad.reshape(n, rows, features),
        n,
        share,
        splits,
    )

    def together(terms):
        terms = terms.reshape(heads, share, rows, HEAD_DIM)
        total = jnp.sum(terms.astype(FLT), axis=1).astype(HALF)
        return total.transpose(1, 0, 2).reshape(rows, width)

    grad_queries = dq.transpose(1, 0, 2).reshape(rows, width)
    layer_grad = grad.transpose(1, 0, 2).reshape(rows, -1)
    return (layer_grad, grad_proj, grad_out, grad_queries, together(dk), together(dv))


def solution(mesh):
    placed = (
        P("seq", "head"),
        P(),
        P(),
        P("seq", None),
        P("seq", "head"),
        P("head", "seq"),
        P("seq", "head"),
        P("seq", "head"),
        P("seq", "head"),
        P("seq", "head"),
    )
    return jax.shard_map(
        body,
        mesh=mesh,
        in_specs=placed,
        out_specs=(
            P("seq", "head"),
            P("seq", "head"),
            P("head", "seq"),
            P("seq", "head"),
            P("seq", "head"),
            P("seq", "head"),
        ),
        check_vma=False,
    )
```

```python
import functools
import math

import jax
import jax.numpy as jnp
from jax import lax
from jax.experimental import pallas as pl
from jax.experimental.pallas import tpu as pltpu
from jax.sharding import PartitionSpec as P

HEAD_DIM = 128
MESH = pl.DeviceIdType.MESH
FLT = jnp.float32
HALF = jnp.bfloat16
ANY = pl.BlockSpec(memory_space=pl.ANY)
VMEM = pl.BlockSpec(memory_space=pltpu.VMEM)
SMEM = pl.BlockSpec(memory_space=pltpu.SMEM)
VMEM_LIMIT = 56 * 1024 * 1024


def greet(axes):
    barrier = pltpu.get_barrier_semaphore()
    count = 0
    for axis, size in axes:
        me = lax.axis_index(axis)
        for k in range(1, size):
            pl.semaphore_signal(
                barrier, inc=1, device_id={axis: lax.rem(me + k, size)}, device_id_type=MESH
            )
        count += size - 1
    pl.semaphore_wait(barrier, count)


def spread(stride, n, source, target, send, recv):
    me = lax.axis_index("seq")
    size = n // stride
    copies = []
    for k in range(1, size):
        dst = lax.rem(me // stride + k, size) * stride + lax.rem(me, stride)
        copy = pltpu.make_async_remote_copy(
            src_ref=source(dst),
            dst_ref=target,
            send_sem=send.at[k],
            recv_sem=recv.at[k],
            device_id={"seq": dst},
            device_id_type=MESH,
        )
        copy.start()
        copies.append(copy)
    own = pltpu.make_async_copy(source(me), target, recv.at[0])
    own.start()
    return copies + [own]


def gather_kernel(n, d_ref, out_ref, send, recv, pair_send, pair_recv):
    me = lax.axis_index("seq")
    chips = n // 2
    chip, core = me // 2, lax.rem(me, 2)
    other = chip * 2 + (1 - core)
    greet((("seq", n),))
    copies = spread(2, n, lambda dst: d_ref, out_ref.at[me], send, recv)

    def pass_on(k, source, slot):
        copy = pltpu.make_async_remote_copy(
            src_ref=source,
            dst_ref=out_ref.at[slot],
            send_sem=pair_send.at[k],
            recv_sem=pair_recv.at[k],
            device_id={"seq": other},
            device_id_type=MESH,
        )
        copy.start()
        return copy

    passed = [pass_on(0, d_ref, me)]
    for k in range(1, chips):
        copies[k - 1].wait_recv()
        slot = lax.rem(chip + chips - k, chips) * 2 + core
        passed.append(pass_on(k, out_ref.at[slot], slot))
    for copy in passed:
        copy.wait()
    for copy in copies[:-1]:
        copy.wait_send()
    copies[-1].wait()


def gather(d_bytes, n):
    chips = n // 2
    return pl.pallas_call(
        functools.partial(gather_kernel, n),
        out_shape=jax.ShapeDtypeStruct((n,) + d_bytes.shape, d_bytes.dtype),
        in_specs=[ANY],
        out_specs=ANY,
        scratch_shapes=[pltpu.SemaphoreType.DMA((chips,))] * 4,
        compiler_params=pltpu.CompilerParams(collective_id=1, has_side_effects=True),
    )(d_bytes)


def middle_kernel(
    n, splits, heads, chunks,
    part, y, q, k, v, o,
    grad, y_all, q_all, k_all, v_all, o_all, oq_all,
    outer_buf, pair_buf, middle_buf, total,
    y_s, y_r, q_s, q_r, k_s, k_r, v_s, v_r, o_s, o_r, p_s, p_r, a_s, a_r, b_s, b_r, c_s, c_r,
):
    me = lax.axis_index("seq")
    z = lax.axis_index("head")
    share = n // heads
    greet((("seq", n), ("head", splits)) if splits == 4 else (("seq", n),))
    rows = part.shape[0] // chunks
    inner = jnp.logical_and(z >= 1, z <= 2)
    outer = jnp.logical_not(inner)
    beside = (z // 2) * 2 + (1 - lax.rem(z, 2))
    across = 3 - z

    def send(source, target, s, r, c, to):
        here = pl.ds(c * rows, rows)
        return pltpu.make_async_remote_copy(
            src_ref=source.at[here],
            dst_ref=target.at[here],
            send_sem=s.at[c],
            recv_sem=r.at[c],
            device_id={"head": to},
            device_id_type=MESH,
        )

    line = splits == 4
    first = [send(part, outer_buf, a_s, a_r, c, beside) for c in range(chunks)]
    second = [send(pair_buf, middle_buf, b_s, b_r, c, across) for c in range(chunks)]
    third = [send(total, total, c_s, c_r, c, beside) for c in range(chunks)]

    if line:

        @pl.when(outer)
        def _():
            for copy in first:
                copy.start()

    width = y.shape[1] // n

    def columns(ref, size, index):
        return ref.at[:, pl.ds(pl.multiple_of(index * size, size), size)]

    copies = spread(share, n, lambda d: columns(q, HEAD_DIM, d // share), q_all.at[me // share], q_s, q_r)
    copies += spread(share, n, lambda d: columns(o, HEAD_DIM, d // share), oq_all.at[me // share], p_s, p_r)
    copies += spread(1, n, lambda d: o, o_all.at[me], o_s, o_r)
    copies += spread(1, n, lambda d: columns(k, HEAD_DIM, d // share), k_all.at[me], k_s, k_r)
    copies += spread(1, n, lambda d: columns(v, HEAD_DIM, d // share), v_all.at[me], v_s, v_r)
    copies += spread(1, n, lambda d: columns(y, width, d), y_all.at[me], y_s, y_r)

    if line:

        @pl.when(inner)
        def _():
            lag = 2
            for step in range(chunks + lag):
                if step < chunks:
                    here = pl.ds(step * rows, rows)
                    first[step].wait_recv()
                    pair_buf[here] = (part[here].astype(FLT) + outer_buf[here].astype(FLT)).astype(HALF)
                    second[step].start()
                if step >= lag:
                    c = step - lag
                    here = pl.ds(c * rows, rows)
                    second[c].wait_recv()
                    total[here] = (pair_buf[here].astype(FLT) + middle_buf[here].astype(FLT)).astype(HALF)
                    third[c].start()
            for c in range(chunks):
                second[c].wait_send()
                third[c].wait_send()

        @pl.when(outer)
        def _():
            for c in range(chunks):
                third[c].wait_recv()
            for c in range(chunks):
                first[c].wait_send()

        grad[...] = total[...]
    else:
        grad[...] = part[...]
    for copy in copies:
        copy.wait()


def middle(part, y, q, k, v, o, n, splits):
    heads = q.shape[1] // HEAD_DIM
    rows = y.shape[0]
    chunks = 8
    block = lambda m, w: jax.ShapeDtypeStruct((m, rows, w), HALF)
    dma = pltpu.SemaphoreType.DMA
    return pl.pallas_call(
        functools.partial(middle_kernel, n, splits, heads, chunks),
        out_shape=(
            jax.ShapeDtypeStruct(part.shape, HALF),
            block(n, y.shape[1] // n),
            block(heads, HEAD_DIM),
            block(n, HEAD_DIM),
            block(n, HEAD_DIM),
            block(n, o.shape[1]),
            block(heads, HEAD_DIM),
        ),
        in_specs=[VMEM] + [ANY] * 5,
        out_specs=[VMEM] + [ANY] * 6,
        scratch_shapes=[pltpu.VMEM(part.shape, HALF)] * 4
        + [dma((n,))] * 12
        + [dma((chunks,))] * 6,
        compiler_params=pltpu.CompilerParams(
            collective_id=2, has_side_effects=True, vmem_limit_bytes=VMEM_LIMIT
        ),
    )(part, y, q, k, v, o)


def scatter_kernel(n, share, a_ref, nat_ref, y, out_ref, proj, nat, sem, send, recv):
    me = lax.axis_index("seq")
    greet((("seq", n),))

    def source(d):
        column = pl.ds(pl.multiple_of(d // share * HEAD_DIM, HEAD_DIM), HEAD_DIM)
        return a_ref.at[:, lax.rem(d, share), :, column]

    copies = spread(1, n, source, out_ref.at[me], send, recv)
    fetch = pltpu.make_async_copy(nat_ref, nat, sem)
    fetch.start()
    fetch.wait()
    tile = 512

    @pl.loop(0, nat.shape[1] // tile)
    def _(i):
        here = pl.ds(pl.multiple_of(i * tile, tile), tile)
        proj[:, here] = lax.dot_general(
            y[...], nat[:, here], (((0,), (0,)), ((), ())), preferred_element_type=FLT
        ).astype(HALF)

    for copy in copies:
        copy.wait()


def scatter(partial, natural, y, n, share):
    slots, rows = partial.shape[0], partial.shape[2]
    return pl.pallas_call(
        functools.partial(scatter_kernel, n, share),
        out_shape=(
            jax.ShapeDtypeStruct((n, slots, rows, HEAD_DIM), HALF),
            jax.ShapeDtypeStruct((y.shape[1], natural.shape[1]), HALF),
        ),
        in_specs=[ANY, ANY, VMEM],
        out_specs=[ANY, VMEM],
        scratch_shapes=[pltpu.VMEM(natural.shape, HALF), pltpu.SemaphoreType.DMA]
        + [pltpu.SemaphoreType.DMA((n,))] * 2,
        compiler_params=pltpu.CompilerParams(
            collective_id=3, has_side_effects=True, vmem_limit_bytes=VMEM_LIMIT
        ),
    )(partial, natural, y)


def return_kernel(
    n, share, per, dq, dk, dv, grad, dq_out, dk_out, dv_out, grad_out, q_s, q_r, k_s, k_r, v_s, v_r, g_s, g_r
):
    me = lax.axis_index("seq")
    c = lax.axis_index("head")
    splits = n // per
    slot = lax.rem(me, per)
    goal = me // per
    base = lax.rem(c + splits - goal, splits)
    barrier = pltpu.get_barrier_semaphore()
    for i in range(splits):
        for k in range(n):
            if i + k > 0:
                pl.semaphore_signal(
                    barrier,
                    inc=1,
                    device_id={"seq": lax.rem(me + k, n), "head": lax.rem(c + i, splits)},
                    device_id_type=MESH,
                )
    pl.semaphore_wait(barrier, n * splits - 1)
    away, shares, own = [], [], []
    for j in range(per):
        dst = base + j * splits
        away.append(jnp.logical_or(dst != me, goal != c))
        shares.append(
            pltpu.make_async_remote_copy(
                src_ref=grad.at[dst],
                dst_ref=grad_out.at[slot],
                send_sem=g_s.at[j],
                recv_sem=g_r.at[slot],
                device_id={"seq": dst, "head": goal},
                device_id_type=MESH,
            )
        )
        own.append(pltpu.make_async_copy(grad.at[dst], grad_out.at[slot], g_r.at[slot]))

    for j in range(per):

        @pl.when(away[j])
        def _():
            shares[j].start()

        @pl.when(jnp.logical_not(away[j]))
        def _():
            own[j].start()

    copies = spread(share, n, lambda d: dq.at[d // share], dq_out.at[me // share], q_s, q_r)
    copies += spread(1, n, lambda d: dk.at[d], dk_out.at[me], k_s, k_r)
    copies += spread(1, n, lambda d: dv.at[d], dv_out.at[me], v_s, v_r)
    for copy in copies:
        copy.wait()

    for j in range(per):

        @pl.when(away[j])
        def _():
            shares[j].wait_send()

    for i in range(per):
        pltpu.make_async_copy(grad.at[0], grad_out.at[i], g_r.at[i]).wait()


def send_back(dq, dk, dv, grad, n, share, splits):
    per = n // splits
    dma = pltpu.SemaphoreType.DMA
    return pl.pallas_call(
        functools.partial(return_kernel, n, share, per),
        out_shape=(
            jax.ShapeDtypeStruct(dq.shape, HALF),
            jax.ShapeDtypeStruct(dk.shape, HALF),
            jax.ShapeDtypeStruct(dv.shape, HALF),
            jax.ShapeDtypeStruct((per,) + grad.shape[1:], HALF),
        ),
        in_specs=[ANY] * 4,
        out_specs=[ANY] * 4,
        scratch_shapes=[dma((n,))] * 6 + [dma((per,))] * 2,
        compiler_params=pltpu.CompilerParams(collective_id=4, has_side_effects=True),
    )(dq, dk, dv, grad)


def fetch_natural(groups, d_ref, nat, sem):
    owners, slots = groups.shape
    size = nat.shape[0] // (owners * slots)

    @pl.loop(0, owners)
    def _(o):
        for j in range(slots):
            g = groups[o, j]
            pltpu.make_async_copy(
                d_ref.at[o, pl.ds(j * size, size)],
                nat.at[pl.ds(pl.multiple_of(g * size, size), size)],
                sem,
            ).start()


def natural_done(nat, sem):
    pltpu.make_async_copy(nat, nat, sem).wait()


def part_kernel(groups, d_ref, w, out, nat_out, nat, sem):
    fetch_natural(groups, d_ref, nat, sem)
    natural_done(nat, sem)
    keep = pltpu.make_async_copy(nat, nat_out, sem)
    keep.start()
    tile = 256

    @pl.loop(0, nat.shape[0] // tile)
    def _(i):
        here = pl.ds(pl.multiple_of(i * tile, tile), tile)
        out[here] = lax.dot_general(
            nat[here], w[...], (((1,), (1,)), ((), ())), preferred_element_type=FLT
        ).astype(HALF)

    keep.wait()


def with_natural(kernel, groups, d_all, other, out_shape):
    nat = (d_all.shape[0] * d_all.shape[1], d_all.shape[2])
    return pl.pallas_call(
        kernel,
        out_shape=(jax.ShapeDtypeStruct(out_shape, HALF), jax.ShapeDtypeStruct(nat, HALF)),
        in_specs=[SMEM, ANY, VMEM],
        out_specs=[VMEM, ANY],
        scratch_shapes=[pltpu.VMEM(nat, HALF), pltpu.SemaphoreType.DMA],
        compiler_params=pltpu.CompilerParams(vmem_limit_bytes=VMEM_LIMIT),
    )(groups, d_all, other)


def attention_kernel(qpos, kpos, q, k, v, o, go, dq, dk, dv, dk_sum, dv_sum):
    j = pl.program_id(0)
    scale = 1.0 / math.sqrt(HEAD_DIM)

    @pl.when(j == 0)
    def _():
        dk_sum[...] = jnp.zeros_like(dk_sum)
        dv_sum[...] = jnp.zeros_like(dv_sum)

    g = jnp.sum(go[:, 0].astype(FLT), axis=0).astype(HALF)
    delta = jnp.sum(g.astype(FLT) * o[0].astype(FLT), axis=1, keepdims=True)
    rowwise = (((1,), (1,)), ((), ()))
    columnwise = (((0,), (0,)), ((), ()))
    s = lax.dot_general(q[0], k[...], rowwise, preferred_element_type=FLT) * scale
    s = jnp.where(kpos[...] <= qpos[0], s, -1e30)
    high = jnp.max(s, axis=1, keepdims=True)
    e = jnp.exp(s - high)
    p = e * (1.0 / jnp.sum(e, axis=1, keepdims=True))
    dp = lax.dot_general(g, v[...], rowwise, preferred_element_type=FLT)
    ds = (p * (dp - delta) * scale).astype(HALF)
    low = p.astype(HALF)
    dq[0] = jnp.dot(ds, k[...], preferred_element_type=FLT).astype(HALF)
    dk_sum[...] += lax.dot_general(ds, q[0], columnwise, preferred_element_type=FLT)
    dv_sum[...] += lax.dot_general(low, g, columnwise, preferred_element_type=FLT)

    @pl.when(j == pl.num_programs(0) - 1)
    def _():
        dk[...] = dk_sum[...].astype(HALF)
        dv[...] = dv_sum[...].astype(HALF)


def attention(qpos, kpos, q, k, v, o, go):
    slots, rows, _ = q.shape
    n = go.shape[0]
    every = k.shape
    block = pl.BlockSpec((1, rows, HEAD_DIM), lambda j: (j, 0, 0))
    whole = pl.BlockSpec(every, lambda j: (0, 0))
    return pl.pallas_call(
        attention_kernel,
        grid=(slots,),
        out_shape=(
            jax.ShapeDtypeStruct(q.shape, HALF),
            jax.ShapeDtypeStruct(every, HALF),
            jax.ShapeDtypeStruct(every, HALF),
        ),
        in_specs=[
            pl.BlockSpec((1, rows, 1), lambda j: (j, 0, 0)),
            pl.BlockSpec(kpos.shape, lambda j: (0, 0)),
            block,
            whole,
            whole,
            block,
            pl.BlockSpec((n, 1, rows, HEAD_DIM), lambda j: (0, j, 0, 0)),
        ],
        out_specs=[block, whole, whole],
        scratch_shapes=[pltpu.VMEM(every, FLT)] * 2,
        compiler_params=pltpu.CompilerParams(vmem_limit_bytes=VMEM_LIMIT),
    )(qpos, kpos, q, k, v, o, go)


def body(d_bytes, owner_groups, block_order, y_in, w_proj, w_out, queries, keys, values, attn_out):
    n = lax.axis_size("seq")
    splits = lax.axis_size("head")
    me = lax.axis_index("seq")
    rows, width = queries.shape
    heads = width // HEAD_DIM
    share = n // heads
    patches = n * rows
    features = w_proj.shape[0]

    d_all = gather(d_bytes, n)
    part, natural = with_natural(part_kernel, owner_groups, d_all, w_proj, (patches, features))
    if splits != 4:
        part = lax.psum(part, "head")
    grad, y_all, q_all, k_all, v_all, o_all, oq_all = middle(
        part, y_in, queries, keys, values, attn_out, n, splits
    )
    partial = lax.dot_general(
        grad, w_out, (((1,), (1,)), ((), ())), preferred_element_type=FLT
    ).astype(HALF)
    go, grad_proj = scatter(
        partial.reshape(heads, share, rows, width), natural, y_all.reshape(patches, features), n, share
    )
    grad_out = lax.dot_general(
        o_all.reshape(patches, width), grad, (((0,), (0,)), ((), ())), preferred_element_type=FLT
    ).astype(HALF)
    pos = block_order[:, None] * rows + jnp.arange(rows, dtype=jnp.int32)[None, :]
    mine = lax.dynamic_index_in_dim(pos.reshape(heads, share, rows), lax.rem(me, share), 1, False)
    dq, dk, dv = attention(
        mine[:, :, None],
        pos.reshape(1, patches),
        q_all,
        k_all.reshape(patches, HEAD_DIM),
        v_all.reshape(patches, HEAD_DIM),
        oq_all,
        go,
    )
    dq, dk, dv, grad = send_back(
        dq,
        dk.reshape(n, rows, HEAD_DIM),
        dv.reshape(n, rows, HEAD_DIM),
        grad.reshape(n, rows, features),
        n,
        share,
        splits,
    )

    def together(terms):
        terms = terms.reshape(heads, share, rows, HEAD_DIM)
        total = jnp.sum(terms.astype(FLT), axis=1).astype(HALF)
        return total.transpose(1, 0, 2).reshape(rows, width)

    grad_queries = dq.transpose(1, 0, 2).reshape(rows, width)
    layer_grad = grad.transpose(1, 0, 2).reshape(rows, -1)
    return (layer_grad, grad_proj, grad_out, grad_queries, together(dk), together(dv))


def solution(mesh):
    placed = (
        P("seq", "head"),
        P(),
        P(),
        P("seq", None),
        P("seq", "head"),
        P("head", "seq"),
        P("seq", "head"),
        P("seq", "head"),
        P("seq", "head"),
        P("seq", "head"),
    )
    return jax.shard_map(
        body,
        mesh=mesh,
        in_specs=placed,
        out_specs=(
            P("seq", "head"),
            P("seq", "head"),
            P("head", "seq"),
            P("seq", "head"),
            P("seq", "head"),
            P("seq", "head"),
        ),
        check_vma=False,
    )
```

```python
import functools
import math

import jax
import jax.numpy as jnp
from jax import lax
from jax.experimental import pallas as pl
from jax.experimental.pallas import tpu as pltpu
from jax.sharding import PartitionSpec as P

HEAD_DIM = 128
MESH = pl.DeviceIdType.MESH
FLT = jnp.float32
HALF = jnp.bfloat16
ANY = pl.BlockSpec(memory_space=pl.ANY)
VMEM = pl.BlockSpec(memory_space=pltpu.VMEM)
SMEM = pl.BlockSpec(memory_space=pltpu.SMEM)
VMEM_LIMIT = 56 * 1024 * 1024


def greet(axes):
    barrier = pltpu.get_barrier_semaphore()
    count = 0
    for axis, size in axes:
        me = lax.axis_index(axis)
        for k in range(1, size):
            pl.semaphore_signal(
                barrier, inc=1, device_id={axis: lax.rem(me + k, size)}, device_id_type=MESH
            )
        count += size - 1
    pl.semaphore_wait(barrier, count)


def spread(stride, n, source, target, send, recv):
    me = lax.axis_index("seq")
    size = n // stride
    copies = []
    for k in range(1, size):
        dst = lax.rem(me // stride + k, size) * stride + lax.rem(me, stride)
        copy = pltpu.make_async_remote_copy(
            src_ref=source(dst),
            dst_ref=target,
            send_sem=send.at[k],
            recv_sem=recv.at[k],
            device_id={"seq": dst},
            device_id_type=MESH,
        )
        copy.start()
        copies.append(copy)
    own = pltpu.make_async_copy(source(me), target, recv.at[0])
    own.start()
    return copies + [own]


def gather_kernel(n, d_ref, out_ref, send, recv, pair_send, pair_recv):
    me = lax.axis_index("seq")
    chips = n // 2
    chip, core = me // 2, lax.rem(me, 2)
    other = chip * 2 + (1 - core)
    greet((("seq", n),))
    copies = spread(2, n, lambda dst: d_ref, out_ref.at[me], send, recv)

    def pass_on(k, source, slot):
        copy = pltpu.make_async_remote_copy(
            src_ref=source,
            dst_ref=out_ref.at[slot],
            send_sem=pair_send.at[k],
            recv_sem=pair_recv.at[k],
            device_id={"seq": other},
            device_id_type=MESH,
        )
        copy.start()
        return copy

    passed = [pass_on(0, d_ref, me)]
    for k in range(1, chips):
        copies[k - 1].wait_recv()
        slot = lax.rem(chip + chips - k, chips) * 2 + core
        passed.append(pass_on(k, out_ref.at[slot], slot))
    for copy in passed:
        copy.wait()
    for copy in copies[:-1]:
        copy.wait_send()
    copies[-1].wait()


def gather(d_bytes, n):
    chips = n // 2
    return pl.pallas_call(
        functools.partial(gather_kernel, n),
        out_shape=jax.ShapeDtypeStruct((n,) + d_bytes.shape, d_bytes.dtype),
        in_specs=[ANY],
        out_specs=ANY,
        scratch_shapes=[pltpu.SemaphoreType.DMA((chips,))] * 4,
        compiler_params=pltpu.CompilerParams(collective_id=1, has_side_effects=True),
    )(d_bytes)


def middle_kernel(
    n, splits, heads, chunks,
    part, y, q, k, v, o,
    grad, y_all, q_all, k_all, v_all, o_all, oq_all,
    outer_buf, pair_buf, middle_buf, total,
    y_s, y_r, q_s, q_r, k_s, k_r, v_s, v_r, o_s, o_r, p_s, p_r, a_s, a_r, b_s, b_r, c_s, c_r,
    fo_s, fo_r, fk_s, fk_r, fv_s, fv_r,
):
    me = lax.axis_index("seq")
    z = lax.axis_index("head")
    share = n // heads
    greet((("seq", n), ("head", splits)) if splits == 4 else (("seq", n),))
    rows = part.shape[0] // chunks
    inner = jnp.logical_and(z >= 1, z <= 2)
    outer = jnp.logical_not(inner)
    beside = (z // 2) * 2 + (1 - lax.rem(z, 2))
    across = 3 - z

    def send(source, target, s, r, c, to):
        here = pl.ds(c * rows, rows)
        return pltpu.make_async_remote_copy(
            src_ref=source.at[here],
            dst_ref=target.at[here],
            send_sem=s.at[c],
            recv_sem=r.at[c],
            device_id={"head": to},
            device_id_type=MESH,
        )

    line = splits == 4
    first = [send(part, outer_buf, a_s, a_r, c, beside) for c in range(chunks)]
    second = [send(pair_buf, middle_buf, b_s, b_r, c, across) for c in range(chunks)]
    third = [send(total, total, c_s, c_r, c, beside) for c in range(chunks)]

    if line:

        @pl.when(outer)
        def _():
            for copy in first:
                copy.start()

    width = y.shape[1] // n

    def columns(ref, size, index):
        return ref.at[:, pl.ds(pl.multiple_of(index * size, size), size)]

    copies = spread(share, n, lambda d: columns(q, HEAD_DIM, d // share), q_all.at[me // share], q_s, q_r)
    copies += spread(share, n, lambda d: columns(o, HEAD_DIM, d // share), oq_all.at[me // share], p_s, p_r)
    chips = n // 2
    chip, core = me // 2, lax.rem(me, 2)
    other = chip * 2 + (1 - core)
    head = me // share
    shared = [
        (o_all, o, lambda d: o, o_s, o_r, fo_s, fo_r),
        (k_all, columns(k, HEAD_DIM, head), lambda d: columns(k, HEAD_DIM, d // share), k_s, k_r, fk_s, fk_r),
        (v_all, columns(v, HEAD_DIM, head), lambda d: columns(v, HEAD_DIM, d // share), v_s, v_r, fv_s, fv_r),
    ]

    def pass_on(source, target, s, r, i):
        copy = pltpu.make_async_remote_copy(
            src_ref=source,
            dst_ref=target,
            send_sem=s.at[i],
            recv_sem=r.at[i],
            device_id={"seq": other},
            device_id_type=MESH,
        )
        copy.start()
        return copy

    between, passed = [], []
    for out, mine, source, s, r, fs, fr in shared:
        between.append(spread(2, n, source, out.at[me], s, r))
        passed.append(pass_on(mine, out.at[me], fs, fr, 0))
    copies += spread(1, n, lambda d: columns(y, width, d), y_all.at[me], y_s, y_r)

    if line:

        @pl.when(inner)
        def _():
            lag = 2
            for step in range(chunks + lag):
                if step < chunks:
                    here = pl.ds(step * rows, rows)
                    first[step].wait_recv()
                    pair_buf[here] = (part[here].astype(FLT) + outer_buf[here].astype(FLT)).astype(HALF)
                    second[step].start()
                if step >= lag:
                    c = step - lag
                    here = pl.ds(c * rows, rows)
                    second[c].wait_recv()
                    total[here] = (pair_buf[here].astype(FLT) + middle_buf[here].astype(FLT)).astype(HALF)
                    third[c].start()
            for c in range(chunks):
                second[c].wait_send()
                third[c].wait_send()

        @pl.when(outer)
        def _():
            for c in range(chunks):
                third[c].wait_recv()
            for c in range(chunks):
                first[c].wait_send()

        grad[...] = total[...]
    else:
        grad[...] = part[...]
    for arrived, (out, _, _, _, _, fs, fr) in zip(between, shared):
        for i in range(1, chips):
            arrived[i - 1].wait_recv()
            slot = lax.rem(chip + chips - i, chips) * 2 + core
            passed.append(pass_on(out.at[slot], out.at[slot], fs, fr, i))
        for copy in arrived[:-1]:
            copy.wait_send()
        arrived[-1].wait()
    for copy in copies + passed:
        copy.wait()


def middle(part, y, q, k, v, o, n, splits):
    heads = q.shape[1] // HEAD_DIM
    rows = y.shape[0]
    chunks = 8
    block = lambda m, w: jax.ShapeDtypeStruct((m, rows, w), HALF)
    dma = pltpu.SemaphoreType.DMA
    return pl.pallas_call(
        functools.partial(middle_kernel, n, splits, heads, chunks),
        out_shape=(
            jax.ShapeDtypeStruct(part.shape, HALF),
            block(n, y.shape[1] // n),
            block(heads, HEAD_DIM),
            block(n, HEAD_DIM),
            block(n, HEAD_DIM),
            block(n, o.shape[1]),
            block(heads, HEAD_DIM),
        ),
        in_specs=[VMEM] + [ANY] * 5,
        out_specs=[VMEM] + [ANY] * 6,
        scratch_shapes=[pltpu.VMEM(part.shape, HALF)] * 4
        + [dma((n,))] * 12
        + [dma((chunks,))] * 6
        + [dma((n // 2,))] * 6,
        compiler_params=pltpu.CompilerParams(
            collective_id=2, has_side_effects=True, vmem_limit_bytes=VMEM_LIMIT
        ),
    )(part, y, q, k, v, o)


def scatter_kernel(n, share, a_ref, nat_ref, y, out_ref, proj, nat, sem, send, recv):
    me = lax.axis_index("seq")
    greet((("seq", n),))

    def source(d):
        column = pl.ds(pl.multiple_of(d // share * HEAD_DIM, HEAD_DIM), HEAD_DIM)
        return a_ref.at[:, lax.rem(d, share), :, column]

    copies = spread(1, n, source, out_ref.at[me], send, recv)
    fetch = pltpu.make_async_copy(nat_ref, nat, sem)
    fetch.start()
    fetch.wait()
    tile = 512

    @pl.loop(0, nat.shape[1] // tile)
    def _(i):
        here = pl.ds(pl.multiple_of(i * tile, tile), tile)
        proj[:, here] = lax.dot_general(
            y[...], nat[:, here], (((0,), (0,)), ((), ())), preferred_element_type=FLT
        ).astype(HALF)

    for copy in copies:
        copy.wait()


def scatter(partial, natural, y, n, share):
    slots, rows = partial.shape[0], partial.shape[2]
    return pl.pallas_call(
        functools.partial(scatter_kernel, n, share),
        out_shape=(
            jax.ShapeDtypeStruct((n, slots, rows, HEAD_DIM), HALF),
            jax.ShapeDtypeStruct((y.shape[1], natural.shape[1]), HALF),
        ),
        in_specs=[ANY, ANY, VMEM],
        out_specs=[ANY, VMEM],
        scratch_shapes=[pltpu.VMEM(natural.shape, HALF), pltpu.SemaphoreType.DMA]
        + [pltpu.SemaphoreType.DMA((n,))] * 2,
        compiler_params=pltpu.CompilerParams(
            collective_id=3, has_side_effects=True, vmem_limit_bytes=VMEM_LIMIT
        ),
    )(partial, natural, y)


def return_kernel(
    n, share, per, dq, dk, dv, grad, dq_out, dk_out, dv_out, grad_out, q_s, q_r, k_s, k_r, v_s, v_r, g_s, g_r
):
    me = lax.axis_index("seq")
    c = lax.axis_index("head")
    splits = n // per
    slot = lax.rem(me, per)
    goal = me // per
    base = lax.rem(c + splits - goal, splits)
    barrier = pltpu.get_barrier_semaphore()
    for i in range(splits):
        for k in range(n):
            if i + k > 0:
                pl.semaphore_signal(
                    barrier,
                    inc=1,
                    device_id={"seq": lax.rem(me + k, n), "head": lax.rem(c + i, splits)},
                    device_id_type=MESH,
                )
    pl.semaphore_wait(barrier, n * splits - 1)
    away, shares, own = [], [], []
    for j in range(per):
        dst = base + j * splits
        away.append(jnp.logical_or(dst != me, goal != c))
        shares.append(
            pltpu.make_async_remote_copy(
                src_ref=grad.at[dst],
                dst_ref=grad_out.at[slot],
                send_sem=g_s.at[j],
                recv_sem=g_r.at[slot],
                device_id={"seq": dst, "head": goal},
                device_id_type=MESH,
            )
        )
        own.append(pltpu.make_async_copy(grad.at[dst], grad_out.at[slot], g_r.at[slot]))

    for j in range(per):

        @pl.when(away[j])
        def _():
            shares[j].start()

        @pl.when(jnp.logical_not(away[j]))
        def _():
            own[j].start()

    copies = spread(share, n, lambda d: dq.at[d // share], dq_out.at[me // share], q_s, q_r)
    copies += spread(1, n, lambda d: dk.at[d], dk_out.at[me], k_s, k_r)
    copies += spread(1, n, lambda d: dv.at[d], dv_out.at[me], v_s, v_r)
    for copy in copies:
        copy.wait()

    for j in range(per):

        @pl.when(away[j])
        def _():
            shares[j].wait_send()

    for i in range(per):
        pltpu.make_async_copy(grad.at[0], grad_out.at[i], g_r.at[i]).wait()


def send_back(dq, dk, dv, grad, n, share, splits):
    per = n // splits
    dma = pltpu.SemaphoreType.DMA
    return pl.pallas_call(
        functools.partial(return_kernel, n, share, per),
        out_shape=(
            jax.ShapeDtypeStruct(dq.shape, HALF),
            jax.ShapeDtypeStruct(dk.shape, HALF),
            jax.ShapeDtypeStruct(dv.shape, HALF),
            jax.ShapeDtypeStruct((per,) + grad.shape[1:], HALF),
        ),
        in_specs=[ANY] * 4,
        out_specs=[ANY] * 4,
        scratch_shapes=[dma((n,))] * 6 + [dma((per,))] * 2,
        compiler_params=pltpu.CompilerParams(collective_id=4, has_side_effects=True),
    )(dq, dk, dv, grad)


def fetch_natural(groups, d_ref, nat, sem):
    owners, slots = groups.shape
    size = nat.shape[0] // (owners * slots)

    @pl.loop(0, owners)
    def _(o):
        for j in range(slots):
            g = groups[o, j]
            pltpu.make_async_copy(
                d_ref.at[o, pl.ds(j * size, size)],
                nat.at[pl.ds(pl.multiple_of(g * size, size), size)],
                sem,
            ).start()


def natural_done(nat, sem):
    pltpu.make_async_copy(nat, nat, sem).wait()


def part_kernel(groups, d_ref, w, out, nat_out, nat, sem):
    fetch_natural(groups, d_ref, nat, sem)
    natural_done(nat, sem)
    keep = pltpu.make_async_copy(nat, nat_out, sem)
    keep.start()
    tile = 256

    @pl.loop(0, nat.shape[0] // tile)
    def _(i):
        here = pl.ds(pl.multiple_of(i * tile, tile), tile)
        out[here] = lax.dot_general(
            nat[here], w[...], (((1,), (1,)), ((), ())), preferred_element_type=FLT
        ).astype(HALF)

    keep.wait()


def with_natural(kernel, groups, d_all, other, out_shape):
    nat = (d_all.shape[0] * d_all.shape[1], d_all.shape[2])
    return pl.pallas_call(
        kernel,
        out_shape=(jax.ShapeDtypeStruct(out_shape, HALF), jax.ShapeDtypeStruct(nat, HALF)),
        in_specs=[SMEM, ANY, VMEM],
        out_specs=[VMEM, ANY],
        scratch_shapes=[pltpu.VMEM(nat, HALF), pltpu.SemaphoreType.DMA],
        compiler_params=pltpu.CompilerParams(vmem_limit_bytes=VMEM_LIMIT),
    )(groups, d_all, other)


def attention_kernel(qpos, kpos, q, k, v, o, go, dq, dk, dv, dk_sum, dv_sum):
    j = pl.program_id(0)
    scale = 1.0 / math.sqrt(HEAD_DIM)

    @pl.when(j == 0)
    def _():
        dk_sum[...] = jnp.zeros_like(dk_sum)
        dv_sum[...] = jnp.zeros_like(dv_sum)

    g = jnp.sum(go[:, 0].astype(FLT), axis=0).astype(HALF)
    delta = jnp.sum(g.astype(FLT) * o[0].astype(FLT), axis=1, keepdims=True)
    rowwise = (((1,), (1,)), ((), ()))
    columnwise = (((0,), (0,)), ((), ()))
    s = lax.dot_general(q[0], k[...], rowwise, preferred_element_type=FLT) * scale
    s = jnp.where(kpos[...] <= qpos[0], s, -1e30)
    high = jnp.max(s, axis=1, keepdims=True)
    e = jnp.exp(s - high)
    p = e * (1.0 / jnp.sum(e, axis=1, keepdims=True))
    dp = lax.dot_general(g, v[...], rowwise, preferred_element_type=FLT)
    ds = (p * (dp - delta) * scale).astype(HALF)
    low = p.astype(HALF)
    dq[0] = jnp.dot(ds, k[...], preferred_element_type=FLT).astype(HALF)
    dk_sum[...] += lax.dot_general(ds, q[0], columnwise, preferred_element_type=FLT)
    dv_sum[...] += lax.dot_general(low, g, columnwise, preferred_element_type=FLT)

    @pl.when(j == pl.num_programs(0) - 1)
    def _():
        dk[...] = dk_sum[...].astype(HALF)
        dv[...] = dv_sum[...].astype(HALF)


def attention(qpos, kpos, q, k, v, o, go):
    slots, rows, _ = q.shape
    n = go.shape[0]
    every = k.shape
    block = pl.BlockSpec((1, rows, HEAD_DIM), lambda j: (j, 0, 0))
    whole = pl.BlockSpec(every, lambda j: (0, 0))
    return pl.pallas_call(
        attention_kernel,
        grid=(slots,),
        out_shape=(
            jax.ShapeDtypeStruct(q.shape, HALF),
            jax.ShapeDtypeStruct(every, HALF),
            jax.ShapeDtypeStruct(every, HALF),
        ),
        in_specs=[
            pl.BlockSpec((1, rows, 1), lambda j: (j, 0, 0)),
            pl.BlockSpec(kpos.shape, lambda j: (0, 0)),
            block,
            whole,
            whole,
            block,
            pl.BlockSpec((n, 1, rows, HEAD_DIM), lambda j: (0, j, 0, 0)),
        ],
        out_specs=[block, whole, whole],
        scratch_shapes=[pltpu.VMEM(every, FLT)] * 2,
        compiler_params=pltpu.CompilerParams(vmem_limit_bytes=VMEM_LIMIT),
    )(qpos, kpos, q, k, v, o, go)


def body(d_bytes, owner_groups, block_order, y_in, w_proj, w_out, queries, keys, values, attn_out):
    n = lax.axis_size("seq")
    splits = lax.axis_size("head")
    me = lax.axis_index("seq")
    rows, width = queries.shape
    heads = width // HEAD_DIM
    share = n // heads
    patches = n * rows
    features = w_proj.shape[0]

    d_all = gather(d_bytes, n)
    part, natural = with_natural(part_kernel, owner_groups, d_all, w_proj, (patches, features))
    if splits != 4:
        part = lax.psum(part, "head")
    grad, y_all, q_all, k_all, v_all, o_all, oq_all = middle(
        part, y_in, queries, keys, values, attn_out, n, splits
    )
    partial = lax.dot_general(
        grad, w_out, (((1,), (1,)), ((), ())), preferred_element_type=FLT
    ).astype(HALF)
    go, grad_proj = scatter(
        partial.reshape(heads, share, rows, width), natural, y_all.reshape(patches, features), n, share
    )
    grad_out = lax.dot_general(
        o_all.reshape(patches, width), grad, (((0,), (0,)), ((), ())), preferred_element_type=FLT
    ).astype(HALF)
    pos = block_order[:, None] * rows + jnp.arange(rows, dtype=jnp.int32)[None, :]
    mine = lax.dynamic_index_in_dim(pos.reshape(heads, share, rows), lax.rem(me, share), 1, False)
    dq, dk, dv = attention(
        mine[:, :, None],
        pos.reshape(1, patches),
        q_all,
        k_all.reshape(patches, HEAD_DIM),
        v_all.reshape(patches, HEAD_DIM),
        oq_all,
        go,
    )
    dq, dk, dv, grad = send_back(
        dq,
        dk.reshape(n, rows, HEAD_DIM),
        dv.reshape(n, rows, HEAD_DIM),
        grad.reshape(n, rows, features),
        n,
        share,
        splits,
    )

    def together(terms):
        terms = terms.reshape(heads, share, rows, HEAD_DIM)
        total = jnp.sum(terms.astype(FLT), axis=1).astype(HALF)
        return total.transpose(1, 0, 2).reshape(rows, width)

    grad_queries = dq.transpose(1, 0, 2).reshape(rows, width)
    layer_grad = grad.transpose(1, 0, 2).reshape(rows, -1)
    return (layer_grad, grad_proj, grad_out, grad_queries, together(dk), together(dv))


def solution(mesh):
    placed = (
        P("seq", "head"),
        P(),
        P(),
        P("seq", None),
        P("seq", "head"),
        P("head", "seq"),
        P("seq", "head"),
        P("seq", "head"),
        P("seq", "head"),
        P("seq", "head"),
    )
    return jax.shard_map(
        body,
        mesh=mesh,
        in_specs=placed,
        out_specs=(
            P("seq", "head"),
            P("seq", "head"),
            P("head", "seq"),
            P("seq", "head"),
            P("seq", "head"),
            P("seq", "head"),
        ),
        check_vma=False,
    )
```
